256 devices in a mesh: row: 16 (over z, core), col: 16 (over x, y).
Axes of the slice: x: 4, y: 4, z: 8, core: 2. Of those that a mesh axis runs over, the one named last changes fastest.
Arguments:
- front_values: float32 [2, 16, 512, 2, 16, 512], P(None, 'row', None, None, 'col'), as said below
- block_pattern: int32 [32, 32], replicated, may hold values from 0 to 1, as said below
- panel_order: int32 [32], replicated, may hold values from 0 to 31, each once
Outputs:
- factor: float32 [2, 16, 512, 2, 16, 512], P(None, 'row', None, None, 'col')
The draws below stay inside these ranges and needn't reach their ends.
Inputs may be any that keep to these rules, and one draw needn't show every extreme that they name: front_values is symmetric, and with block_pattern applied it is positive definite. `block_pattern`: symmetric, with ones on the diagonal. `panel_order`: each of 0 to 31 once; the first 3 entries are the block columns eliminated, in order.
All inputs are finite; a program needn't handle non-finite values.
Results may differ from the reference program's by a relative error of at most 0.0001.
Values sent between devices are 32-bit elements; how exact they have to be, the bound alone decides.
A program may use at most 128 MiB of HBM per device.

```python
import math
import jax
import jax.numpy as jnp
from jax import lax

BS = 512
NBLK = 32
PANELS = 3
N_ROW = 16
N_COL = 16


def draw_front_values(key, part):
    key = jax.random.fold_in(key, 11)
    entry_key, diag_key, scale_key = jax.random.split(key, 3)
    order_full = NBLK * BS
    spread = 2.3 / math.sqrt(order_full)
    raw_values = jnp.clip(jax.random.normal(entry_key, (order_full, order_full), jnp.float32), -4.0, 4.0)
    scales = jnp.exp(jax.random.uniform(scale_key, (order_full,), jnp.float32, math.log(0.8), math.log(1.25)))
    diagonal = jax.random.uniform(diag_key, (order_full,), jnp.float32, 5.0, 6.0)
    symmetric = (raw_values + raw_values.T) * (spread / math.sqrt(2.0))
    matrix_full = (symmetric + jnp.diag(diagonal)) * scales[:, None] * scales[None, :]
    return matrix_full.reshape(NBLK // N_ROW, N_ROW, BS, NBLK // N_COL, N_COL, BS)


def draw_block_pattern(key, part):
    key = jax.random.fold_in(key, 23)
    picks = jax.random.randint(key, (NBLK, NBLK), 0, 10)
    upper = jnp.triu((picks < 7).astype(jnp.int32), 1)
    return upper + upper.T + jnp.eye(NBLK, dtype=jnp.int32)


def setup_inputs(seed: int = 0) -> dict:
    splits = jax.random.split(jax.random.key(seed), 4)
    return {
        "front_values": draw_front_values(jax.random.fold_in(splits[3], 71), 0),
        "block_pattern": draw_block_pattern(jax.random.fold_in(splits[3], 71), 0),
        "panel_order": jax.random.permutation(splits[2], NBLK).astype(jnp.int32),
    }


precise = lax.Precision.HIGHEST

def product(first, second):
    return jnp.dot(first.astype(jnp.float32), second.astype(jnp.float32), precision=precise, preferred_element_type=jnp.float32)

def reference(front_values, block_pattern, panel_order):
    order_full = NBLK * BS
    blocked = front_values.reshape(NBLK, BS, NBLK, BS) * block_pattern.astype(jnp.float32)[:, None, :, None]
    matrix_now = blocked.reshape(order_full, order_full)
    identity = jnp.eye(BS, dtype=jnp.float32)
    finished = jnp.zeros((NBLK,), jnp.float32)
    block_ids = jnp.arange(NBLK, dtype=jnp.int32)
    for section_index in range(PANELS):
        pivot_block = panel_order[section_index].astype(jnp.int32)
        offset = (pivot_block * BS).astype(jnp.int32)
        is_pivot = (block_ids == pivot_block).astype(jnp.float32)
        remaining = jnp.repeat(1.0 - finished - is_pivot, BS)
        diag_block = lax.dynamic_slice(matrix_now, (offset, offset), (BS, BS))
        lower_factor = jnp.linalg.cholesky(diag_block)
        inverse = jax.scipy.linalg.solve_triangular(lower_factor, identity, lower=True)
        column_raw = lax.dynamic_slice_in_dim(matrix_now, offset, BS, 1)
        row_raw = lax.dynamic_slice_in_dim(matrix_now, offset, BS, 0)
        column_panel = product(column_raw, inverse.T)
        row_panel = product(inverse, row_raw)
        left_factor = column_panel * remaining[:, None]
        right_factor = row_panel * remaining[None, :]
        matrix_now = matrix_now - product(left_factor, right_factor)
        old_column = lax.dynamic_slice_in_dim(matrix_now, offset, BS, 1)
        new_column = jnp.where(remaining[:, None] > 0, column_panel, old_column)
        matrix_now = lax.dynamic_update_slice_in_dim(matrix_now, new_column, offset, 1)
        old_row = lax.dynamic_slice_in_dim(matrix_now, offset, BS, 0)
        new_row = jnp.where(remaining[None, :] > 0, row_panel, old_row)
        matrix_now = lax.dynamic_update_slice_in_dim(matrix_now, new_row, offset, 0)
        matrix_now = lax.dynamic_update_slice(matrix_now, lower_factor, (offset, offset))
        finished = finished + is_pivot
    return matrix_now.reshape(NBLK // N_ROW, N_ROW, BS, NBLK // N_COL, N_COL, BS)
```

```python
import functools

import jax
import jax.numpy as jnp
from jax import lax
from jax.experimental import pallas as pl
from jax.experimental.pallas import tpu as pltpu
from jax.sharding import PartitionSpec as P

PANELS = 3
BS = 512
PAIRS = ((0, 0), (1, 0), (1, 1), (2, 0), (2, 1), (2, 2))
MESH = pl.DeviceIdType.MESH


def remote(src, dst, sems, index, row, col):
    return pltpu.make_async_remote_copy(
        src_ref=src,
        dst_ref=dst,
        send_sem=sems[0].at[index],
        recv_sem=sems[1].at[index],
        device_id=(row, col),
        device_id_type=MESH,
    )


class Plane:
    def __init__(self, cand, out, out_base, first, first_sum, second, sems, base, rows, place):
        self.cand, self.out, self.out_base = cand, out, out_base
        self.first, self.first_sum, self.second = first, first_sum, second
        self.sems, self.base, self.rows = sems, base, rows
        self.row, self.x, self.y = place
        self.copies = {}

    def peers(self, half, step):
        along_x = (half == 0) == (step == 0)
        for d in (1, 2, 3):
            if along_x:
                px, py = lax.rem(self.x + d, 4), self.y
                to = px
            else:
                px, py = self.x, lax.rem(self.y + d, 4)
                to = py
            yield d, to, px * 4 + py

    def mine(self, half):
        return (self.x, self.y) if half == 0 else (self.y, self.x)

    def start(self, phase):
        big, small = self.rows // 8, self.rows // 32
        for half in (0, 1):
            top = half * (self.rows // 2)
            a, b = self.mine(half)
            copies = []
            step = 0 if phase in (0, 3) else 1
            for d, to, col in self.peers(half, step):
                index = self.base + (phase * 2 + half) * 3 + d - 1
                if phase == 0:
                    src = self.cand.at[pl.ds(pl.multiple_of(top + to * big, 8), big), :]
                    dst = self.first.at[half, d - 1]
                elif phase == 1:
                    src = self.first_sum.at[half, pl.ds(pl.multiple_of(to * small, 8), small), :]
                    dst = self.second.at[half, d - 1]
                elif phase == 2:
                    at = pl.multiple_of(self.out_base + top + a * big + b * small, 8)
                    src = dst = self.out.at[pl.ds(at, small), :]
                else:
                    at = pl.multiple_of(self.out_base + top + a * big, 8)
                    src = dst = self.out.at[pl.ds(at, big), :]
                copy = remote(src, dst, self.sems, index, self.row, col)
                copy.start()
                copies.append(copy)
            self.copies[phase, half] = copies

    def finish(self, phase):
        big, small = self.rows // 8, self.rows // 32
        for half in (0, 1):
            for copy in self.copies[phase, half]:
                copy.wait_recv()
            top = half * (self.rows // 2)
            a, b = self.mine(half)
            if phase == 0:
                own = self.cand[pl.ds(pl.multiple_of(top + a * big, 8), big), :]
                self.first_sum[half] = (
                    own + self.first[half, 0] + self.first[half, 1] + self.first[half, 2]
                )
            elif phase == 1:
                own = self.first_sum[half, pl.ds(pl.multiple_of(b * small, 8), small), :]
                at = pl.multiple_of(self.out_base + top + a * big + b * small, 8)
                self.out[pl.ds(at, small), :] = (
                    own + self.second[half, 0] + self.second[half, 1] + self.second[half, 2]
                )

    def drain(self):
        for copies in self.copies.values():
            for copy in copies:
                copy.wait_send()


def share_kernel(flag_ref, m, p_out, q_out, d_out,
                 p_cand, q_cand, p_first, p_sum, p_second,
                 d_cand, d_first, d_sum, d_second, sib, ring, send_sem, recv_sem):
    row, col = lax.axis_index("row"), lax.axis_index("col")
    z, core = row // 2, lax.rem(row, 2)
    x, y = col // 4, lax.rem(col, 4)
    sems = (send_sem, recv_sem)
    sibling = z * 2 + (1 - core)
    up = lax.rem(z + 1, 8) * 2 + core
    down = lax.rem(z + 7, 8) * 2 + core

    barrier = pltpu.get_barrier_semaphore()
    places = [(sibling, col), (up, col), (down, col)]
    for d in (1, 2, 3):
        places.append((row, lax.rem(x + d, 4) * 4 + y))
        places.append((row, x * 4 + lax.rem(y + d, 4)))
    for place in places:
        pl.semaphore_signal(barrier, inc=1, device_id=place, device_id_type=MESH)

    for t in range(PANELS):
        p0, p1 = flag_ref[t * 2], flag_ref[t * 2 + 1]
        q0, q1 = flag_ref[6 + t * 2], flag_ref[6 + t * 2 + 1]

        def build(i, _, t=t, p0=p0, p1=p1, q0=q0, q1=q1):
            at = pl.multiple_of(i * 64, 64)
            p_cand[pl.ds(t * 1024 + at, 64), :] = (
                m[pl.ds(at, 64), :BS] * p0 + m[pl.ds(at, 64), BS:] * p1
            )
            return 0

        lax.fori_loop(0, 16, build, 0)

        def build_row(i, _, t=t, p0=p0, p1=p1, q0=q0, q1=q1):
            at = pl.multiple_of(i * 64, 64)
            both = m[pl.ds(at, 64), :] * q0 + m[pl.ds(512 + at, 64), :] * q1
            q_cand[pl.ds(t * 1024 + at, 64), :] = both[:, :BS]
            q_cand[pl.ds(t * 1024 + 512 + at, 64), :] = both[:, BS:]
            return 0

        lax.fori_loop(0, 8, build_row, 0)

    pl.semaphore_wait(barrier, 9)

    plane = Plane(p_cand, p_out, 0, p_first, p_sum, p_second, sems, 0, 3072, (row, x, y))
    plane.start(0)

    half_rows = 1536
    mine = pl.multiple_of(core * half_rows, 8)
    other = pl.multiple_of((1 - core) * half_rows, 8)
    swap = remote(q_cand.at[pl.ds(other, half_rows), :], sib, sems, 48, sibling, col)
    swap.start()
    swap.wait_recv()

    def merge(i, _):
        at = pl.multiple_of(i * 64, 64)
        sib[pl.ds(at, 64), :] = sib[pl.ds(at, 64), :] + q_cand[pl.ds(mine + at, 64), :]
        return 0

    lax.fori_loop(0, 24, merge, 0)

    def part(number, way):
        return pl.ds(pl.multiple_of(number * 192 + way * 96, 8), 96)

    pending = []
    for step in range(7):
        copies = []
        for way in (0, 1):
            number = lax.rem(z + 7 - step, 8) if way == 0 else lax.rem(z + 1 + step, 8)
            copy = remote(sib.at[part(number, way), :], ring.at[way, step], sems,
                          50 + step * 2 + way, up if way == 0 else down, col)
            copy.start()
            copies.append(copy)
        for way in (0, 1):
            copies[way].wait_recv()
            number = lax.rem(z + 6 - step + 8, 8) if way == 0 else lax.rem(z + 2 + step, 8)
            if step < 6:
                sib[part(number, way), :] = sib[part(number, way), :] + ring[way, step]
            else:
                at = pl.multiple_of(mine + z * 192 + way * 96, 8)
                q_out[pl.ds(at, 96), :] = sib[part(number, way), :] + ring[way, step]
        pending += copies
        if step == 5:
            plane.finish(0)
            plane.start(1)
    plane.finish(1)
    plane.start(2)
    for step in range(7):
        copies = []
        for way in (0, 1):
            number = lax.rem(z + 8 - step, 8) if way == 0 else lax.rem(z + step, 8)
            at = pl.multiple_of(mine + number * 192 + way * 96, 8)
            copy = remote(q_out.at[pl.ds(at, 96), :], q_out.at[pl.ds(at, 96), :], sems,
                          64 + step * 2 + way, up if way == 0 else down, col)
            copy.start()
            copies.append(copy)
        if step == 1:
            plane.finish(2)
            plane.start(3)
        for way in (0, 1):
            copies[way].wait_recv()
        pending += copies
    final = remote(q_out.at[pl.ds(mine, half_rows), :], q_out.at[pl.ds(mine, half_rows), :],
                   sems, 49, sibling, col)
    final.start()
    final.wait_recv()

    for b, (t, s) in enumerate(PAIRS):
        w0, w1 = flag_ref[s * 2], flag_ref[s * 2 + 1]

        def pick(i, _, t=t, b=b, w0=w0, w1=w1):
            at = pl.multiple_of(i * 64, 64)
            src = pl.multiple_of(t * 1024 + core * 256 + at, 8)
            d_cand[pl.ds(b * 256 + at, 64), :] = (
                q_out[pl.ds(src, 64), :] * w0 + q_out[pl.ds(src + 512, 64), :] * w1
            )
            return 0

        lax.fori_loop(0, 4, pick, 0)
    cross = Plane(d_cand, d_out, mine, d_first, d_sum, d_second, sems, 24, 1536, (row, x, y))
    plane.finish(3)
    for phase in range(4):
        cross.start(phase)
        cross.finish(phase)
    last = remote(d_out.at[pl.ds(mine, half_rows), :], d_out.at[pl.ds(mine, half_rows), :],
                  sems, 78, sibling, col)
    last.start()
    last.wait_recv()
    for copy in pending + [swap, final, last]:
        copy.wait_send()
    plane.drain()
    cross.drain()


def share(m, flags):
    f32 = jnp.float32
    whole = jax.ShapeDtypeStruct((3072, BS), f32)
    vmem = pl.BlockSpec(memory_space=pltpu.VMEM)
    return pl.pallas_call(
        share_kernel,
        out_shape=(whole, whole, whole),
        in_specs=[pl.BlockSpec(memory_space=pltpu.SMEM), vmem],
        out_specs=(vmem, vmem, vmem),
        scratch_shapes=[
            pltpu.VMEM((3072, BS), f32),
            pltpu.VMEM((3072, BS), f32),
            pltpu.VMEM((2, 3, 384, BS), f32),
            pltpu.VMEM((2, 384, BS), f32),
            pltpu.VMEM((2, 3, 96, BS), f32),
            pltpu.VMEM((1536, BS), f32),
            pltpu.VMEM((2, 3, 192, BS), f32),
            pltpu.VMEM((2, 192, BS), f32),
            pltpu.VMEM((2, 3, 48, BS), f32),
            pltpu.VMEM((1536, BS), f32),
            pltpu.VMEM((2, 7, 96, BS), f32),
            pltpu.SemaphoreType.DMA((80,)),
            pltpu.SemaphoreType.DMA((80,)),
        ],
        compiler_params=pltpu.CompilerParams(
            collective_id=0, has_side_effects=True, vmem_limit_bytes=60 * 1024 * 1024
        ),
    )(flags, m)


def split(v):
    high = v.astype(jnp.bfloat16)
    low = (v - high.astype(jnp.float32)).astype(jnp.bfloat16)
    return high, low


def dot_first(a, b):
    return lax.dot_general(a, b, (((0,), (0,)), ((), ())), preferred_element_type=jnp.float32)


STRIP = 16


def invert_kernel(a_ref, u_ref, w_ref, m):
    m[:, :BS] = a_ref[...]
    rows = lax.broadcasted_iota(jnp.int32, (BS, BS), 0)
    cols = lax.broadcasted_iota(jnp.int32, (BS, BS), 1)
    m[:, BS:] = jnp.where(rows == cols, 1.0, 0.0)
    sub = lax.broadcasted_iota(jnp.int32, (STRIP, 128), 0)
    lane = lax.broadcasted_iota(jnp.int32, (STRIP, 128), 1)
    tile = (STRIP, 128)

    def outer(o, _):
        r0 = pl.multiple_of(o * 128, 128)
        for i in range(128 // STRIP):
            rr = r0 + i * STRIP
            strip = [m[pl.ds(rr, STRIP), pl.ds(k * 128, 128)] for k in range(8)]
            diag = m[pl.ds(rr, STRIP), pl.ds(r0, 128)]
            column = [
                jnp.broadcast_to(diag[:, i * STRIP + j : i * STRIP + j + 1], tile)
                for j in range(STRIP)
            ]
            for j in range(STRIP):
                scale = lax.rsqrt(jnp.broadcast_to(column[j][j : j + 1, :], tile))
                solved = column[j] * scale
                below = jnp.where(sub > j, solved, 0.0)
                for k in range(j + 1, STRIP):
                    column[k] = column[k] - below * jnp.broadcast_to(solved[k : k + 1, :], tile)
                for k in range(8):
                    row = jnp.broadcast_to(strip[k][j : j + 1, :], tile) * scale
                    strip[k] = jnp.where(sub == j, row, strip[k] - below * row)
            for k in range(4):
                strip[k] = jnp.where(lane + k * 128 >= sub + rr, strip[k], 0.0)
            for k in range(8):
                m[pl.ds(rr, STRIP), pl.ds(k * 128, 128)] = strip[k]
            if i < 128 // STRIP - 1:
                rest = 128 - (i + 1) * STRIP
                ph, plow = split(jnp.concatenate(strip, axis=1))
                dh, dl = split(m[pl.ds(rr, STRIP), pl.ds(r0, 128)])
                left = jnp.concatenate([dh, dh, dl], axis=0)
                right = jnp.concatenate([ph, plow, ph], axis=0)
                change = dot_first(left, right)
                below_rows = pl.ds(rr + STRIP, rest)
                m[below_rows, :] = m[below_rows, :] - change[(i + 1) * STRIP :, :]
        ph, plow = split(m[pl.ds(r0, 128), :])
        for k in range(4):

            @pl.when(k > o)
            def _():
                lh, ll = ph[:, k * 128 : (k + 1) * 128], plow[:, k * 128 : (k + 1) * 128]
                left = jnp.concatenate([lh, lh, ll], axis=0)
                right = jnp.concatenate([ph, plow, ph], axis=0)
                at = pl.ds(k * 128, 128)
                m[at, :] = m[at, :] - dot_first(left, right)

        return 0

    lax.fori_loop(0, 4, outer, 0)
    u_ref[...] = m[:, :BS]
    w_ref[...] = m[:, BS:]


def invert(a):
    vmem = pl.BlockSpec(memory_space=pltpu.VMEM)
    return pl.pallas_call(
        invert_kernel,
        out_shape=(jax.ShapeDtypeStruct((BS, BS), jnp.float32),) * 2,
        in_specs=[vmem],
        out_specs=(vmem, vmem),
        scratch_shapes=[pltpu.VMEM((BS, 2 * BS), jnp.float32)],
        compiler_params=pltpu.CompilerParams(vmem_limit_bytes=32 * 1024 * 1024),
    )(a)


def product(first, second):
    return jnp.dot(first, second, precision=lax.Precision.HIGH, preferred_element_type=jnp.float32)


def per_device(front_values, block_pattern, panel_order):
    row, col = lax.axis_index("row"), lax.axis_index("col")
    pattern = lax.dynamic_slice(
        block_pattern.reshape(2, 16, 2, 16), (0, row, 0, col), (2, 1, 2, 1)
    ).reshape(2, 2).astype(jnp.float32)
    m = (front_values.reshape(2, BS, 2, BS) * pattern[:, None, :, None]).reshape(2 * BS, 2 * BS)
    pivots = panel_order[:PANELS]
    slots = jnp.arange(2, dtype=jnp.int32)
    here_col = (pivots[:, None] == slots[None, :] * 16 + col).astype(jnp.float32).reshape(6)
    here_row = (pivots[:, None] == slots[None, :] * 16 + row).astype(jnp.float32).reshape(6)
    p_all, q_all, d_all = share(m, jnp.concatenate([here_col, here_row]))
    p_all = p_all.reshape(PANELS, 2 * BS, BS)
    q_all = q_all.reshape(PANELS, 2, BS, BS).transpose(0, 2, 1, 3).reshape(PANELS, BS, 2 * BS)
    d_all = d_all.reshape(2, 6, BS // 2, BS).transpose(1, 0, 2, 3).reshape(6, BS, BS)
    d = {pair: d_all[i] for i, pair in enumerate(PAIRS)}
    crossing = {}
    lowers, lefts, rights = [], [], []
    for t in range(PANELS):
        upper, inverse = invert(d[t, t])
        lowers.append(upper.T)
        for s in range(t + 1, PANELS):
            crossing[t, s] = product(inverse, d[s, t].T)
        for a in range(t + 1, PANELS):
            for b in range(t + 1, a + 1):
                d[a, b] = d[a, b] - product(crossing[t, a].T, crossing[t, b])
        left, right = p_all[t], q_all[t]
        for s in range(t):
            left = left - product(lefts[s], crossing[s, t])
            right = right - product(crossing[s, t].T, rights[s])
        lefts.append(product(left, inverse.T))
        rights.append(product(inverse, right))
    updated = m
    row_ids = slots * 16 + row
    col_ids = slots * 16 + col
    row_turn = jnp.where(row_ids[:, None] == pivots[None, :], 0, 3)
    row_turn = jnp.min(row_turn + jnp.arange(3)[None, :] * (row_turn == 0), axis=1)
    col_turn = jnp.where(col_ids[:, None] == pivots[None, :], 0, 3)
    col_turn = jnp.min(col_turn + jnp.arange(3)[None, :] * (col_turn == 0), axis=1)
    updated = m - product(jnp.concatenate(lefts, axis=1), jnp.concatenate(rights, axis=0))
    blocks = []
    for a in range(2):
        line = []
        for b in range(2):
            block = updated[a * BS : (a + 1) * BS, b * BS : (b + 1) * BS]
            for t in range(PANELS):
                left = lefts[t][a * BS : (a + 1) * BS]
                right = rights[t][:, b * BS : (b + 1) * BS]
                block = jnp.where((col_turn[b] == t) & (row_turn[a] > t), left, block)
                block = jnp.where((row_turn[a] == t) & (col_turn[b] > t), right, block)
                block = jnp.where((row_turn[a] == t) & (col_turn[b] == t), lowers[t], block)
            line.append(block)
        blocks.append(jnp.concatenate(line, axis=1))
    return jnp.concatenate(blocks, axis=0).reshape(front_values.shape)


def solution(mesh):
    return jax.shard_map(
        per_device,
        mesh=mesh,
        in_specs=(P(None, "row", None, None, "col", None), P(), P()),
        out_specs=P(None, "row", None, None, "col", None),
        check_vma=False,
    )
```

```python
import jax
import jax.numpy as jnp
from jax import lax
from jax.experimental import pallas as pl
from jax.experimental.pallas import tpu as pltpu
from jax.sharding import PartitionSpec as P

PANELS = 3
BS = 512
STRIP = 16
SEMAPHORES = 192
GROUPS = (((0, 0),), ((1, 0), (1, 1), (2, 0), (2, 1), (2, 2)))
MESH = pl.DeviceIdType.MESH
F32 = jnp.float32


def rows8(start, size):
    return pl.ds(pl.multiple_of(start, 8), size)


def split(v):
    high = v.astype(jnp.bfloat16)
    low = (v - high.astype(F32)).astype(jnp.bfloat16)
    return high, low


def contract(a, b, axis_a, axis_b):
    return lax.dot_general(
        a, b, (((axis_a,), (axis_b,)), ((), ())), preferred_element_type=F32
    )


def product(a, b, axis_a, axis_b):
    ah, al = split(a)
    bh, bl = split(b)
    return (
        contract(ah, bh, axis_a, axis_b)
        + contract(ah, bl, axis_a, axis_b)
        + contract(al, bh, axis_a, axis_b)
    )


class Links:
    def __init__(self, send_sem, recv_sem):
        self.send_sem, self.recv_sem = send_sem, recv_sem
        self.made = []

    def copy(self, src, dst, place):
        index = len(self.made)
        assert index < SEMAPHORES

        def make():
            return pltpu.make_async_remote_copy(
                src_ref=src(),
                dst_ref=dst(),
                send_sem=self.send_sem.at[index],
                recv_sem=self.recv_sem.at[index],
                device_id=place,
                device_id_type=MESH,
            )

        self.made.append(make)
        return make

    def drain(self):
        for make in self.made:
            make().wait_send()


class Line:
    def __init__(self, links, row, x, y, along_x):
        self.links = links
        self.me = x if along_x else y

        def place(d):
            if along_x:
                return (row, lax.rem(x + d, 4) * 4 + y)
            return (row, x * 4 + lax.rem(y + d, 4))

        self.places = {d: place(d) for d in (1, 2, 3)}
        self.spot = {d: lax.rem(self.me + d, 4) for d in range(4)}

    def scatter_direct(self, piece, buffers):
        copies = [
            self.links.copy(
                lambda d=d: piece(self.spot[d]), lambda d=d: buffers.at[d - 1], self.places[d]
            )
            for d in (1, 2, 3)
        ]
        return copies

    def gather_direct(self, piece):
        return [
            self.links.copy(
                lambda: piece(self.me), lambda: piece(self.me), self.places[d]
            )
            for d in (1, 2, 3)
        ]

    def scatter_ring(self, piece, half, near, far):
        far_copies = [
            self.links.copy(
                lambda w=w: half(piece(self.spot[2]), w),
                lambda w=w: far.at[w],
                self.places[1 if w == 0 else 3],
            )
            for w in (0, 1)
        ]
        near_copies = [
            self.links.copy(
                lambda w=w: piece(self.spot[1 if w == 0 else 3]),
                lambda w=w: near.at[w],
                self.places[1 if w == 0 else 3],
            )
            for w in (0, 1)
        ]
        return far_copies, near_copies

    def gather_ring(self, own, piece, half):
        near_copies = [
            self.links.copy(own, lambda: piece(self.me), self.places[d]) for d in (1, 3)
        ]
        far_copies = [
            self.links.copy(
                lambda w=w: half(piece(self.spot[3 if w == 0 else 1]), w),
                lambda w=w: half(piece(self.spot[3 if w == 0 else 1]), w),
                self.places[1 if w == 0 else 3],
            )
            for w in (0, 1)
        ]
        return near_copies, far_copies


def start(copies):
    for make in copies:
        make().start()


def arrive(copies):
    for make in copies:
        make().wait_recv()


def half_rows(ref, way):
    rows = ref.shape[-2]
    at = pl.ds(way * (rows // 2), rows // 2)
    return ref.at[:, at, :] if len(ref.shape) == 3 else ref.at[at, :]


def crossing_path(links, lines, sibling, z, core, col, x, y, count, cand, sib, first,
                  first_sum, second, slices, pieces, chosen, out):
    rows = count * 256
    big, small = rows // 8, rows // 32
    swap = [links.copy(lambda: cand.at[1 - core], lambda: sib, sibling)]
    spots = ((x, y), (y, x))

    def level1(h):
        return lambda k: sib.at[rows8(h * (rows // 2) + k * big, big), :]

    def level2(h):
        return lambda k: first_sum.at[h, rows8(k * small, small), :]

    ph0 = [lines[h].scatter_direct(level1(h), first.at[h]) for h in (0, 1)]
    ph1 = [lines[1 - h].scatter_direct(level2(h), second.at[h]) for h in (0, 1)]

    def zpiece(k, ref=slices):
        lanes = pl.ds(pl.multiple_of(lax.rem(k, 4) * 128, 128), 128)
        return ref.at[rows8((k // 4) * small, small), lanes]

    zs = {d: lax.rem(z + d, 8) for d in range(8)}
    zscatter = [
        links.copy(lambda d=d: zpiece(zs[d]), lambda d=d: pieces.at[d - 1], (zs[d] * 2 + core, col))
        for d in range(1, 8)
    ]
    zgather = [
        links.copy(lambda: zpiece(z, chosen), lambda: zpiece(z, chosen), (zs[d] * 2 + core, col))
        for d in range(1, 8)
    ]

    def out1(h):
        return lambda k: out.at[core, rows8(h * (rows // 2) + k * big, big), :]

    def out2(h):
        a = spots[h][0]
        return lambda k: out.at[core, rows8(h * (rows // 2) + a * big + k * small, small), :]

    ph2 = [lines[1 - h].gather_direct(out2(h)) for h in (0, 1)]
    ph3 = [lines[h].gather_direct(out1(h)) for h in (0, 1)]
    back = [links.copy(lambda: out.at[core], lambda: out.at[core], sibling)]

    def e0():
        start(swap)

    def e1():
        arrive(swap)
        sib[...] = sib[...] + cand[core]
        for h in (0, 1):
            start(ph0[h])

    def e2():
        for h in (0, 1):
            arrive(ph0[h])
            own = sib[rows8(h * (rows // 2) + spots[h][0] * big, big), :]
            first_sum[h] = own + first[h, 0] + first[h, 1] + first[h, 2]
            start(ph1[h])

    def e3():
        for h in (0, 1):
            arrive(ph1[h])
            own = first_sum[h, rows8(spots[h][1] * small, small), :]
            slices[h * small : (h + 1) * small, :] = (
                own + second[h, 0] + second[h, 1] + second[h, 2]
            )
        start(zscatter)

    def e4():
        arrive(zscatter)
        at = rows8((z // 4) * small, small)
        lanes = pl.ds(pl.multiple_of(lax.rem(z, 4) * 128, 128), 128)
        total = slices[at, lanes]
        for d in range(7):
            total = total + pieces[d]
        chosen[at, lanes] = total
        start(zgather)

    def e5():
        arrive(zgather)
        for h in (0, 1):
            a, b = spots[h]
            out[core, rows8(h * (rows // 2) + a * big + b * small, small), :] = chosen[
                h * small : (h + 1) * small, :
            ]
            start(ph2[h])

    def e6():
        for h in (0, 1):
            arrive(ph2[h])
            start(ph3[h])

    def e7():
        for h in (0, 1):
            arrive(ph3[h])
        start(back)

    def e8():
        arrive(back)

    return [e0, e1, e2, e3, e4, e5, e6, e7, e8]


def front_kernel(pattern_ref, order_ref, m, c_row, c_col, u_out, w_out,
                 p_cand, p_far, p_near, p_far2, p_near2, x_cand, x_sib, x_ring, slices,
                 d_bufs, work, inv_h, inv_l, cross_h, cross_l, own_sem, send_sem, recv_sem):
    row, col = lax.axis_index("row"), lax.axis_index("col")
    z, core = row // 2, lax.rem(row, 2)
    x, y = col // 4, lax.rem(col, 4)
    sibling = (z * 2 + (1 - core), col)
    links = Links(send_sem, recv_sem)
    line_x = Line(links, row, x, y, True)
    line_y = Line(links, row, x, y, False)
    lines = (line_x, line_y)
    zs = {d: lax.rem(z + d, 8) for d in range(8)}

    barrier = pltpu.get_barrier_semaphore()
    places = [sibling] + [(zs[d] * 2 + core, col) for d in range(1, 8)]
    places += [line.places[d] for line in lines for d in (1, 2, 3)]
    for place in places:
        pl.semaphore_signal(barrier, inc=1, device_id=place, device_id_type=MESH)

    def flag(test):
        return jnp.where(test, 1.0, 0.0).astype(F32)

    row_ids, col_ids = (row, 16 + row), (col, 16 + col)
    present = {
        (a, b): flag(pattern_ref[row_ids[a], col_ids[b]] > 0) for a in (0, 1) for b in (0, 1)
    }
    in_row = {(t, a): flag(order_ref[t] == row_ids[a]) for t in range(PANELS) for a in (0, 1)}
    in_col = {(t, b): flag(order_ref[t] == col_ids[b]) for t in range(PANELS) for b in (0, 1)}

    def tile(a, b, u, n, k):
        return m[pl.ds((a * BS + u) * 8 + b * 4 + k, n, stride=8), :]

    def build_crossing(groups):
        for half in (0, 1):

            def body(i, _, half=half):
                for k in range(4):
                    tiles = {
                        (a, b): tile(a, b, half * 256 + i * 64, 64, k)
                        for a in (0, 1)
                        for b in (0, 1)
                    }
                    for g in groups:
                        for n, (t, s) in enumerate(GROUPS[g]):
                            total = jnp.zeros((64, 128), F32)
                            for a, b in tiles:
                                weight = in_row[t, a] * in_col[s, b] * present[a, b]
                                total = total + tiles[a, b] * weight
                            at = rows8(n * 256 + i * 64, 64)
                            d_bufs[g][0][half, at, k * 128 : (k + 1) * 128] = total
                return 0

            lax.fori_loop(0, 4, body, 0)

    def build_columns():
        def body(i, _):
            for a in (0, 1):
                for k in range(4):
                    left, right = tile(a, 0, i * 64, 64, k), tile(a, 1, i * 64, 64, k)
                    for t in range(PANELS):
                        p_cand[t, rows8(a * BS + i * 64, 64), k * 128 : (k + 1) * 128] = (
                            left * (in_col[t, 0] * present[a, 0])
                            + right * (in_col[t, 1] * present[a, 1])
                        )
            return 0

        lax.fori_loop(0, 8, body, 0)

    def build_rows():
        def body(i, _):
            lanes = pl.ds(pl.multiple_of(i * 128, 128), 128)
            for b in (0, 1):
                for k in range(4):
                    top, low = tile(0, b, i * 128, 128, k), tile(1, b, i * 128, 128, k)
                    for t in range(PANELS):
                        both = top * (in_row[t, 0] * present[0, b])
                        both = both + low * (in_row[t, 1] * present[1, b])
                        x_cand[t, b * BS + k * 128 : b * BS + (k + 1) * 128, lanes] = both.T
            return 0

        lax.fori_loop(0, 4, body, 0)

    d_paths = [
        crossing_path(links, lines, sibling, z, core, col, x, y, len(GROUPS[g]), *d_bufs[g])
        for g in range(2)
    ]
    d_out = [d_bufs[g][-1] for g in range(2)]

    spots = ((x, y), (y, x))

    def p_piece(h):
        return lambda k: p_cand.at[:, rows8(h * BS + k * 128, 128), :]

    def p_piece2(h):
        a = spots[h][0]
        return lambda k: p_cand.at[:, rows8(h * BS + a * 128 + k * 32, 32), :]

    p_level1 = [lines[h].scatter_ring(p_piece(h), half_rows, p_near.at[h], p_far.at[h]) for h in (0, 1)]
    p_level2 = [
        lines[1 - h].scatter_ring(p_piece2(h), half_rows, p_near2.at[h], p_far2.at[h])
        for h in (0, 1)
    ]

    def add_far(h, line, base, size, far):
        for w, d in ((0, 1), (1, 3)):
            at = rows8(base + line.spot[d] * size + w * (size // 2), size // 2)
            p_cand[:, at, :] = p_cand[:, at, :] + far[h, w]

    def add_near(h, line, base, size, near):
        at = rows8(base + line.me * size, size)
        p_cand[:, at, :] = p_cand[:, at, :] + near[h, 0] + near[h, 1]

    def p0():
        for h in (0, 1):
            start(p_level1[h][0])

    def p1():
        for h in (0, 1):
            arrive(p_level1[h][0])
            add_far(h, lines[h], h * BS, 128, p_far)
            start(p_level1[h][1])

    def p2():
        for h in (0, 1):
            arrive(p_level1[h][1])
            add_near(h, lines[h], h * BS, 128, p_near)
            start(p_level2[h][0])

    def p3():
        for h in (0, 1):
            arrive(p_level2[h][0])
            add_far(h, lines[1 - h], h * BS + spots[h][0] * 128, 32, p_far2)
            start(p_level2[h][1])

    def p4():
        for h in (0, 1):
            arrive(p_level2[h][1])
            at = rows8(h * BS + spots[h][0] * 128 + spots[h][1] * 32, 32)
            slices[:, h * 32 : (h + 1) * 32, :] = (
                p_cand[:, at, :] + p_near2[h, 0] + p_near2[h, 1]
            )

    p_path = [p0, p1, p2, p3, p4]

    up, down = (zs[1] * 2 + core, col), (zs[7] * 2 + core, col)
    x_swap = [
        links.copy(lambda: x_cand.at[:, rows8((1 - core) * BS, BS), :], lambda: x_sib, sibling)
    ]

    def x_piece(k, first=0, size=64):
        return x_sib.at[:, rows8(k * 64 + first, size), :]

    x_steps = []
    for i in range(4):
        size = 32 if i == 0 else 64
        x_steps.append(
            [
                links.copy(
                    lambda w=w, i=i, size=size: x_piece(
                        zs[4 - i if w == 0 else 4 + i], 32 * w if i == 0 else 0, size
                    ),
                    lambda w=w, i=i, size=size: x_ring.at[w, i, :, pl.ds(0, size), :],
                    up if w == 0 else down,
                )
                for w in (0, 1)
            ]
        )

    def x0():
        start(x_swap)

    def x1():
        arrive(x_swap)
        x_sib[...] = x_sib[...] + x_cand[:, rows8(core * BS, BS), :]
        start(x_steps[0])

    def x_next(i):
        def run():
            arrive(x_steps[i - 1])
            first, size = (32, 32) if i == 1 else (0, 64)
            for w in (0, 1):
                number = zs[4 - i if w == 0 else 4 + i]
                at = rows8(number * 64 + first * w, size)
                x_sib[:, at, :] = x_sib[:, at, :] + x_ring[w, i - 1, :, :size, :]
            start(x_steps[i])

        return run

    def x5():
        arrive(x_steps[3])
        slices[:, 64:, :] = x_sib[:, rows8(z * 64, 64), :] + x_ring[0, 3] + x_ring[1, 3]

    x_path = [x0, x1, x_next(1), x_next(2), x_next(3), x5]

    def gather_path(first_panel, count, sem):
        panels = pl.ds(first_panel, count)

        def c_piece(h):
            return lambda k: c_row.at[panels, rows8(h * BS + k * 128, 128), :]

        def c_piece2(h):
            a = spots[h][0]
            return lambda k: c_row.at[panels, rows8(h * BS + a * 128 + k * 32, 32), :]

        def own_rows(h):
            return lambda: slices.at[panels, pl.ds(h * 32, 32), :]

        level2 = [
            lines[1 - h].gather_ring(own_rows(h), c_piece2(h), half_rows) for h in (0, 1)
        ]
        level1 = [
            lines[h].gather_ring(lambda h=h: c_piece(h)(lines[h].me), c_piece(h), half_rows)
            for h in (0, 1)
        ]

        def y_piece(k, first=0, size=64):
            return c_col.at[panels, rows8(core * BS + k * 64 + first, size), :]

        y_own = lambda: slices.at[panels, pl.ds(64, 64), :]
        y_steps = []
        for i in range(4):
            copies = []
            for w in (0, 1):
                first, size = (32 * w, 32) if i == 3 else (0, 64)
                number = zs[(8 - i) % 8 if w == 0 else i]

                def dst(number=number, first=first, size=size):
                    return y_piece(number, first, size)

                copies.append(links.copy(y_own if i == 0 else dst, dst, up if w == 0 else down))
            y_steps.append(copies)
        mine = lambda: c_col.at[panels, rows8(core * BS, BS), :]
        y_back = [links.copy(mine, mine, sibling)]

        def keep(n):
            if n < 2:
                src, dst = own_rows(n)(), c_piece2(n)(spots[n][1])
            else:
                src, dst = y_own(), y_piece(z)
            return pltpu.make_async_copy(src, dst, own_sem.at[sem + n])

        def r0():
            for h in (0, 1):
                keep(h).start()
                start(level2[h][0])

        def r1():
            for h in (0, 1):
                arrive(level2[h][0])
                start(level2[h][1])

        def r2():
            for h in (0, 1):
                keep(h).wait()
                arrive(level2[h][1])
                start(level1[h][0])

        def r3():
            for h in (0, 1):
                arrive(level1[h][0])
                start(level1[h][1])

        def r4():
            for h in (0, 1):
                arrive(level1[h][1])

        def y0():
            keep(2).start()
            start(y_steps[0])

        def y_next(i):
            def run():
                arrive(y_steps[i - 1])
                start(y_steps[i])

            return run

        def y4():
            keep(2).wait()
            arrive(y_steps[3])
            start(y_back)

        def y5():
            arrive(y_back)

        return [r0, r1, r2, r3, r4], [y0, y_next(1), y_next(2), y_next(3), y4, y5]

    ra, ya = gather_path(0, 1, 0)
    rb, yb = gather_path(1, 2, 3)

    sub = lax.broadcasted_iota(jnp.int32, (STRIP, 128), 0)
    lane = lax.broadcasted_iota(jnp.int32, (STRIP, 128), 1)
    shape = (STRIP, 128)

    def strip_step(r0, i):
        rr = pl.multiple_of(r0 + i * STRIP, STRIP)
        strip = [work[pl.ds(rr, STRIP), pl.ds(k * 128, 128)] for k in range(8)]
        diag = work[pl.ds(rr, STRIP), pl.ds(r0, 128)]
        column = [
            jnp.broadcast_to(diag[:, i * STRIP + j : i * STRIP + j + 1], shape)
            for j in range(STRIP)
        ]
        for j in range(STRIP):
            scale = lax.rsqrt(jnp.broadcast_to(column[j][j : j + 1, :], shape))
            solved = column[j] * scale
            below = jnp.where(sub > j, solved, 0.0)
            for k in range(j + 1, STRIP):
                column[k] = column[k] - below * jnp.broadcast_to(solved[k : k + 1, :], shape)
            for k in range(8):
                line = jnp.broadcast_to(strip[k][j : j + 1, :], shape) * scale
                strip[k] = jnp.where(sub == j, line, strip[k] - below * line)
        for k in range(4):
            strip[k] = jnp.where(lane + k * 128 >= sub + rr, strip[k], 0.0)
        for k in range(8):
            work[pl.ds(rr, STRIP), pl.ds(k * 128, 128)] = strip[k]
        if i < 128 // STRIP - 1:
            ph, plow = split(jnp.concatenate(strip, axis=1))
            dh, dl = split(work[pl.ds(rr, STRIP), pl.ds(r0, 128)])
            left = jnp.concatenate([dh, dh, dl], axis=0)
            right = jnp.concatenate([ph, plow, ph], axis=0)
            change = contract(left, right, 0, 0)
            at = pl.ds(rr + STRIP, 128 - (i + 1) * STRIP)
            work[at, :] = work[at, :] - change[(i + 1) * STRIP :, :]

    def factor(events):
        eye_row = lax.broadcasted_iota(jnp.int32, (64, 128), 0)
        eye_lane = lax.broadcasted_iota(jnp.int32, (64, 128), 1)
        for i in range(8):
            work[i * 64 : (i + 1) * 64, BS:] = jnp.zeros((64, BS), F32)
            first = (i // 2) * 128
            work[i * 64 : (i + 1) * 64, BS + first : BS + first + 128] = jnp.where(
                eye_row + (i % 2) * 64 == eye_lane, 1.0, 0.0
            )

        def outer(o, _):
            r0 = pl.multiple_of(o * 128, 128)
            for i in range(128 // STRIP):
                if i % 4 == 0:
                    for k in range(4):
                        todo = events[k * 2 + i // 4]
                        if todo:

                            @pl.when(o == k)
                            def _(todo=todo):
                                for event in todo:
                                    event()

                strip_step(r0, i)
            ph, plow = split(work[pl.ds(r0, 128), :])
            for k in range(1, 4):

                @pl.when(k > o)
                def _(k=k):
                    lh, ll = ph[:, k * 128 : (k + 1) * 128], plow[:, k * 128 : (k + 1) * 128]
                    left = jnp.concatenate([lh, lh, ll], axis=0)
                    right = jnp.concatenate([ph, plow, ph], axis=0)
                    at = pl.ds(k * 128, 128)
                    work[at, :] = work[at, :] - contract(left, right, 0, 0)

            return 0

        lax.fori_loop(0, 4, outer, 0)

    def piece(g, n, i):
        return d_out[g][i // 2, n * 256 + (i % 2) * 128 : n * 256 + (i % 2) * 128 + 128, :]

    def save(t):
        copies = [pltpu.make_async_copy(work.at[:, pl.ds(0, BS)], u_out.at[t], own_sem.at[6 + t])]
        if t == 2:
            copies.append(pltpu.make_async_copy(work.at[:, pl.ds(BS, BS)], w_out, own_sem.at[9]))
        return copies

    def keep_factor(t):
        for copy in save(t):
            copy.start()
        if t < 2:
            for i in range(4):
                at = pl.ds(i * 128, 128)
                inv_h[t, at, :], inv_l[t, at, :] = split(work[at, BS:])

    def solve_crossing(n, t, source):
        for i in range(4):
            bh, bl = split(source(i))
            part = (
                contract(inv_h[t], bh, 1, 1)
                + contract(inv_h[t], bl, 1, 1)
                + contract(inv_l[t], bh, 1, 1)
            )
            lanes = pl.ds(i * 128, 128)
            cross_h[n, :, lanes], cross_l[n, :, lanes] = split(part)

    def pair(first, second, i):
        lanes = pl.ds(i * 128, 128)
        ah, al = cross_h[first, :, lanes], cross_l[first, :, lanes]
        return (
            contract(ah, cross_h[second], 0, 0)
            + contract(ah, cross_l[second], 0, 0)
            + contract(al, cross_h[second], 0, 0)
        )

    def thin(rows, high, low, axis):
        ah, al = split(rows)
        return contract(ah, high, 1, axis) + contract(ah, low, 1, axis) + contract(al, high, 1, axis)

    build_crossing((0,))
    pl.semaphore_wait(barrier, len(places))
    d0, d1 = d_paths
    px, xx = p_path, x_path
    d0[0]()
    build_crossing((1,))
    d0[1]()
    d1[0]()
    build_rows()
    d0[2]()
    xx[0]()
    d1[1]()
    build_columns()
    d0[3]()
    d0[4]()
    d0[5]()
    xx[1]()
    d1[2]()
    d0[6]()
    d1[3]()
    d0[7]()
    px[0]()
    d0[8]()
    for i in range(4):
        work[i * 128 : (i + 1) * 128, :BS] = piece(0, 0, i)
    factor(
        [
            [d1[4], xx[2]],
            [],
            [d1[5]],
            [d1[6]],
            [px[1], xx[3]],
            [d1[7]],
            [],
            [d1[8], xx[4]],
        ]
    )
    keep_factor(0)
    solve_crossing(0, 0, lambda i: piece(1, 0, i))
    for copy in save(0):
        copy.wait()
    for i in range(4):
        work[i * 128 : (i + 1) * 128, :BS] = piece(1, 1, i) - pair(0, 0, i)

    def first_panel():
        slices[0] = thin(slices[0], inv_h[0], inv_l[0], 1)
        ra[0]()
        ya[0]()

    factor(
        [
            [px[2], xx[5]],
            [px[3]],
            [px[4], first_panel],
            [ra[1]],
            [ya[1]],
            [ra[2]],
            [ya[2]],
            [ra[3]],
        ]
    )
    keep_factor(1)
    ya[3]()
    solve_crossing(1, 0, lambda i: piece(1, 2, i))
    solve_crossing(2, 1, lambda i: piece(1, 3, i) - pair(1, 0, i))
    slices[1] = thin(
        slices[1] - thin(slices[0], cross_h[0], cross_l[0], 0), inv_h[1], inv_l[1], 1
    )
    slices[2] = (
        slices[2]
        - thin(slices[0], cross_h[1], cross_l[1], 0)
        - thin(slices[1], cross_h[2], cross_l[2], 0)
    )
    rb[0]()
    yb[0]()
    for copy in save(1):
        copy.wait()
    for i in range(4):
        work[i * 128 : (i + 1) * 128, :BS] = piece(1, 4, i) - pair(1, 1, i) - pair(2, 2, i)
    factor(
        [
            [],
            [rb[1]],
            [yb[1]],
            [rb[2], ra[4]],
            [yb[2], ya[4]],
            [],
            [yb[3]],
            [rb[3], ya[5]],
        ]
    )
    keep_factor(2)
    yb[4]()
    rb[4]()
    yb[5]()
    for copy in save(2):
        copy.wait()
    links.drain()


def eliminate(pattern, order, m):
    vmem = pl.BlockSpec(memory_space=pltpu.VMEM)
    whole = pl.BlockSpec(memory_space=pl.ANY)
    smem = pl.BlockSpec(memory_space=pltpu.SMEM)
    d_shapes = []
    for group in GROUPS:
        rows = len(group) * 256
        d_shapes.append(
            (
                pltpu.VMEM((2, rows, BS), F32),
                pltpu.VMEM((rows, BS), F32),
                pltpu.VMEM((2, 3, rows // 8, BS), F32),
                pltpu.VMEM((2, rows // 8, BS), F32),
                pltpu.VMEM((2, 3, rows // 32, BS), F32),
                pltpu.VMEM((rows // 16, BS), F32),
                pltpu.VMEM((7, rows // 32, 128), F32),
                pltpu.VMEM((rows // 16, BS), F32),
                pltpu.VMEM((2, rows, BS), F32),
            )
        )
    return pl.pallas_call(
        front_kernel,
        out_shape=(
            jax.ShapeDtypeStruct((PANELS, 2 * BS, BS), F32),
            jax.ShapeDtypeStruct((PANELS, 2 * BS, BS), F32),
            jax.ShapeDtypeStruct((PANELS, BS, BS), F32),
            jax.ShapeDtypeStruct((BS, BS), F32),
        ),
        in_specs=[smem, smem, vmem],
        out_specs=(whole, whole, whole, whole),
        scratch_shapes=[
            pltpu.VMEM((PANELS, 2 * BS, BS), F32),
            pltpu.VMEM((2, 2, PANELS, 64, BS), F32),
            pltpu.VMEM((2, 2, PANELS, 128, BS), F32),
            pltpu.VMEM((2, 2, PANELS, 16, BS), F32),
            pltpu.VMEM((2, 2, PANELS, 32, BS), F32),
            pltpu.VMEM((PANELS, 2 * BS, BS), F32),
            pltpu.VMEM((PANELS, BS, BS), F32),
            pltpu.VMEM((2, 4, PANELS, 64, BS), F32),
            pltpu.VMEM((PANELS, 128, BS), F32),
            tuple(d_shapes),
            pltpu.VMEM((BS, 2 * BS), F32),
            pltpu.VMEM((2, BS, BS), jnp.bfloat16),
            pltpu.VMEM((2, BS, BS), jnp.bfloat16),
            pltpu.VMEM((3, BS, BS), jnp.bfloat16),
            pltpu.VMEM((3, BS, BS), jnp.bfloat16),
            pltpu.SemaphoreType.DMA((10,)),
            pltpu.SemaphoreType.DMA((SEMAPHORES,)),
            pltpu.SemaphoreType.DMA((SEMAPHORES,)),
        ],
        compiler_params=pltpu.CompilerParams(
            collective_id=0, has_side_effects=True, vmem_limit_bytes=62 * 1024 * 1024
        ),
    )(pattern, order, m)


def update_kernel(pattern_ref, order_ref, m, c_row, c_col, u_all, w_last, out, high, low):
    for side, ref in enumerate((c_row, c_col)):
        for t in range(2):
            high[side, t], low[side, t] = split(ref[t])
        last = product(ref[2], w_last[...], 1, 1)
        ref_last = last
        high[side, 2], low[side, 2] = split(ref_last)

    row, col = lax.axis_index("row"), lax.axis_index("col")
    row_ids, col_ids = (row, 16 + row), (col, 16 + col)

    def turn(number):
        found = jnp.int32(PANELS)
        for t in reversed(range(PANELS)):
            found = jnp.where(order_ref[t] == number, t, found)
        return found

    def tile_rows(a, b, k, u=0, n=BS):
        return pl.ds((a * BS + u) * 8 + b * 4 + k, n, stride=8)

    def put(a, b, value):
        for k in range(4):
            out[tile_rows(a, b, k), :] = value[:, k * 128 : (k + 1) * 128]

    for a in (0, 1):
        for b in (0, 1):
            ra, cb = turn(row_ids[a]), turn(col_ids[b])
            rows, cols = pl.ds(a * BS, BS), pl.ds(b * BS, BS)

            @pl.when((ra == 3) & (cb == 3))
            def _(a=a, b=b, rows=rows, cols=cols):
                total = jnp.zeros((BS, BS), F32)
                for t in range(PANELS):
                    ch, cl = high[0, t, rows, :], low[0, t, rows, :]
                    rh, rl = high[1, t, cols, :], low[1, t, cols, :]
                    total = total + contract(ch, rh, 1, 1)
                    total = total + contract(ch, rl, 1, 1)
                    total = total + contract(cl, rh, 1, 1)
                present = pattern_ref[row_ids[a], col_ids[b]].astype(F32)
                for k in range(4):
                    at = tile_rows(a, b, k)
                    old = m[at, :] * present
                    out[at, :] = old - total[:, k * 128 : (k + 1) * 128]

            def solved(side, t, at):
                return high[side, t, at, :].astype(F32) + low[side, t, at, :].astype(F32)

            for t in range(PANELS):

                @pl.when((ra == t) & (cb == t))
                def _(a=a, b=b, t=t):
                    put(a, b, u_all[t].T)

                @pl.when((cb == t) & (ra > t))
                def _(a=a, b=b, t=t, rows=rows):
                    put(a, b, solved(0, t, rows))

                @pl.when((ra == t) & (cb > t))
                def _(a=a, b=b, t=t, cols=cols):
                    put(a, b, solved(1, t, cols).T)


def update(pattern, order, m, c_row, c_col, u_all, w_last):
    vmem = pl.BlockSpec(memory_space=pltpu.VMEM)
    smem = pl.BlockSpec(memory_space=pltpu.SMEM)
    return pl.pallas_call(
        update_kernel,
        out_shape=jax.ShapeDtypeStruct(m.shape, F32),
        in_specs=[smem, smem] + [vmem] * 5,
        out_specs=vmem,
        scratch_shapes=[
            pltpu.VMEM((2, PANELS, 2 * BS, BS), jnp.bfloat16),
            pltpu.VMEM((2, PANELS, 2 * BS, BS), jnp.bfloat16),
        ],
        compiler_params=pltpu.CompilerParams(vmem_limit_bytes=50 * 1024 * 1024),
    )(pattern, order, m, c_row, c_col, u_all, w_last)


def per_device(front_values, block_pattern, panel_order):
    m = front_values.reshape(8192, 128)
    solved = eliminate(block_pattern, panel_order, m)
    return update(block_pattern, panel_order, m, *solved).reshape(front_values.shape)


def solution(mesh):
    return jax.shard_map(
        per_device,
        mesh=mesh,
        in_specs=(P(None, "row", None, None, "col", None), P(), P()),
        out_specs=P(None, "row", None, None, "col", None),
        check_vma=False,
    )
```

```python
import jax
import jax.numpy as jnp
from jax import lax
from jax.experimental import pallas as pl
from jax.experimental.pallas import tpu as pltpu
from jax.sharding import PartitionSpec as P

PANELS = 3
BS = 512
STRIP = 32
SEMAPHORES = 256
GROUPS = (((0, 0),), ((1, 0), (1, 1)), ((2, 0), (2, 1), (2, 2)))
MESH = pl.DeviceIdType.MESH
F32 = jnp.float32


def rows8(start, size):
    return pl.ds(pl.multiple_of(start, 8), size)


def split(v):
    high = v.astype(jnp.bfloat16)
    low = (v - high.astype(F32)).astype(jnp.bfloat16)
    return high, low


def contract(a, b, axis_a, axis_b):
    return lax.dot_general(
        a, b, (((axis_a,), (axis_b,)), ((), ())), preferred_element_type=F32
    )


def product(a, b, axis_a, axis_b):
    ah, al = split(a)
    bh, bl = split(b)
    return (
        contract(ah, bh, axis_a, axis_b)
        + contract(ah, bl, axis_a, axis_b)
        + contract(al, bh, axis_a, axis_b)
    )


class Links:
    def __init__(self, send_sem, recv_sem):
        self.send_sem, self.recv_sem = send_sem, recv_sem
        self.made = []

    def copy(self, src, dst, place):
        index = len(self.made)
        assert index < SEMAPHORES

        def make():
            return pltpu.make_async_remote_copy(
                src_ref=src(),
                dst_ref=dst(),
                send_sem=self.send_sem.at[index],
                recv_sem=self.recv_sem.at[index],
                device_id=place,
                device_id_type=MESH,
            )

        self.made.append(make)
        return make

    def drain(self):
        for make in self.made:
            make().wait_send()


class Line:
    def __init__(self, links, row, x, y, along_x):
        self.links = links
        self.me = x if along_x else y

        def place(d):
            if along_x:
                return (row, lax.rem(x + d, 4) * 4 + y)
            return (row, x * 4 + lax.rem(y + d, 4))

        self.places = {d: place(d) for d in (1, 2, 3)}
        self.spot = {d: lax.rem(self.me + d, 4) for d in range(4)}

    def scatter_direct(self, piece, buffers):
        copies = [
            self.links.copy(
                lambda d=d: piece(self.spot[d]), lambda d=d: buffers.at[d - 1], self.places[d]
            )
            for d in (1, 2, 3)
        ]
        return copies

    def gather_direct(self, piece):
        return [
            self.links.copy(
                lambda: piece(self.me), lambda: piece(self.me), self.places[d]
            )
            for d in (1, 2, 3)
        ]

    def scatter_ring(self, piece, half, near, far):
        far_copies = [
            self.links.copy(
                lambda w=w: half(piece(self.spot[2]), w),
                lambda w=w: far.at[w],
                self.places[1 if w == 0 else 3],
            )
            for w in (0, 1)
        ]
        near_copies = [
            self.links.copy(
                lambda w=w: piece(self.spot[1 if w == 0 else 3]),
                lambda w=w: near.at[w],
                self.places[1 if w == 0 else 3],
            )
            for w in (0, 1)
        ]
        return far_copies, near_copies

    def gather_ring(self, own, piece, half):
        near_copies = [
            self.links.copy(own, lambda: piece(self.me), self.places[d]) for d in (1, 3)
        ]
        far_copies = [
            self.links.copy(
                lambda w=w: half(piece(self.spot[3 if w == 0 else 1]), w),
                lambda w=w: half(piece(self.spot[3 if w == 0 else 1]), w),
                self.places[1 if w == 0 else 3],
            )
            for w in (0, 1)
        ]
        return near_copies, far_copies


def start(copies):
    for make in copies:
        make().start()


def arrive(copies):
    for make in copies:
        make().wait_recv()


def half_rows(ref, way):
    rows = ref.shape[-2]
    at = pl.ds(way * (rows // 2), rows // 2)
    return ref.at[:, at, :] if len(ref.shape) == 3 else ref.at[at, :]


def crossing_path(links, lines, sibling, z, core, col, x, y, count, cand, sib, first,
                  first_sum, second, slices, pieces, chosen, out):
    rows = count * 256
    big, small = rows // 8, rows // 32
    swap = [links.copy(lambda: cand.at[1 - core], lambda: sib, sibling)]
    spots = ((x, y), (y, x))

    def level1(h):
        return lambda k: sib.at[rows8(h * (rows // 2) + k * big, big), :]

    def level2(h):
        return lambda k: first_sum.at[h, rows8(k * small, small), :]

    ph0 = [lines[h].scatter_direct(level1(h), first.at[h]) for h in (0, 1)]
    ph1 = [lines[1 - h].scatter_direct(level2(h), second.at[h]) for h in (0, 1)]

    def zpiece(k, ref=slices):
        lanes = pl.ds(pl.multiple_of(lax.rem(k, 4) * 128, 128), 128)
        return ref.at[rows8((k // 4) * small, small), lanes]

    zs = {d: lax.rem(z + d, 8) for d in range(8)}
    zscatter = [
        links.copy(lambda d=d: zpiece(zs[d]), lambda d=d: pieces.at[d - 1], (zs[d] * 2 + core, col))
        for d in range(1, 8)
    ]
    zgather = [
        links.copy(lambda: zpiece(z, chosen), lambda: zpiece(z, chosen), (zs[d] * 2 + core, col))
        for d in range(1, 8)
    ]

    def out1(h):
        return lambda k: out.at[core, rows8(h * (rows // 2) + k * big, big), :]

    def out2(h):
        a = spots[h][0]
        return lambda k: out.at[core, rows8(h * (rows // 2) + a * big + k * small, small), :]

    ph2 = [lines[1 - h].gather_direct(out2(h)) for h in (0, 1)]
    ph3 = [lines[h].gather_direct(out1(h)) for h in (0, 1)]
    back = [links.copy(lambda: out.at[core], lambda: out.at[core], sibling)]

    def e0():
        start(swap)

    def e1():
        arrive(swap)
        sib[...] = sib[...] + cand[core]
        for h in (0, 1):
            start(ph0[h])

    def e2():
        for h in (0, 1):
            arrive(ph0[h])
            own = sib[rows8(h * (rows // 2) + spots[h][0] * big, big), :]
            first_sum[h] = own + first[h, 0] + first[h, 1] + first[h, 2]
            start(ph1[h])

    def e3():
        for h in (0, 1):
            arrive(ph1[h])
            own = first_sum[h, rows8(spots[h][1] * small, small), :]
            slices[h * small : (h + 1) * small, :] = (
                own + second[h, 0] + second[h, 1] + second[h, 2]
            )
        start(zscatter)

    def e4():
        arrive(zscatter)
        at = rows8((z // 4) * small, small)
        lanes = pl.ds(pl.multiple_of(lax.rem(z, 4) * 128, 128), 128)
        total = slices[at, lanes]
        for d in range(7):
            total = total + pieces[d]
        chosen[at, lanes] = total
        start(zgather)

    def e5():
        arrive(zgather)
        for h in (0, 1):
            a, b = spots[h]
            out[core, rows8(h * (rows // 2) + a * big + b * small, small), :] = chosen[
                h * small : (h + 1) * small, :
            ]
            start(ph2[h])

    def e6():
        for h in (0, 1):
            arrive(ph2[h])
            start(ph3[h])

    def e7():
        for h in (0, 1):
            arrive(ph3[h])
        start(back)

    def e8():
        arrive(back)

    return [e0, e1, e2, e3, e4, e5, e6, e7, e8]


def front_kernel(pattern_ref, order_ref, m, c_row, c_col, u_out, w_out,
                 p_cand, p_far, p_near, p_far2, p_near2, x_cand, x_sib, x_ring, slices,
                 d_bufs, work, inv_h, inv_l, cross_h, cross_l, own_sem, send_sem, recv_sem):
    row, col = lax.axis_index("row"), lax.axis_index("col")
    z, core = row // 2, lax.rem(row, 2)
    x, y = col // 4, lax.rem(col, 4)
    sibling = (z * 2 + (1 - core), col)
    links = Links(send_sem, recv_sem)
    line_x = Line(links, row, x, y, True)
    line_y = Line(links, row, x, y, False)
    lines = (line_x, line_y)
    zs = {d: lax.rem(z + d, 8) for d in range(8)}

    barrier = pltpu.get_barrier_semaphore()
    places = [sibling] + [(zs[d] * 2 + core, col) for d in range(1, 8)]
    places += [line.places[d] for line in lines for d in (1, 2, 3)]
    for place in places:
        pl.semaphore_signal(barrier, inc=1, device_id=place, device_id_type=MESH)

    def flag(test):
        return jnp.where(test, 1.0, 0.0).astype(F32)

    row_ids, col_ids = (row, 16 + row), (col, 16 + col)
    present = {
        (a, b): flag(pattern_ref[row_ids[a], col_ids[b]] > 0) for a in (0, 1) for b in (0, 1)
    }
    in_row = {(t, a): flag(order_ref[t] == row_ids[a]) for t in range(PANELS) for a in (0, 1)}
    in_col = {(t, b): flag(order_ref[t] == col_ids[b]) for t in range(PANELS) for b in (0, 1)}

    def tile(a, b, u, n, k):
        return m[pl.ds((a * BS + u) * 8 + b * 4 + k, n, stride=8), :]

    def build_crossing(groups):
        for half in (0, 1):

            def body(i, _, half=half):
                for k in range(4):
                    tiles = {
                        (a, b): tile(a, b, half * 256 + i * 64, 64, k)
                        for a in (0, 1)
                        for b in (0, 1)
                    }
                    for g in groups:
                        for n, (t, s) in enumerate(GROUPS[g]):
                            total = jnp.zeros((64, 128), F32)
                            for a, b in tiles:
                                weight = in_row[t, a] * in_col[s, b] * present[a, b]
                                total = total + tiles[a, b] * weight
                            at = rows8(n * 256 + i * 64, 64)
                            d_bufs[g][0][half, at, k * 128 : (k + 1) * 128] = total
                return 0

            lax.fori_loop(0, 4, body, 0)

    def build_columns():
        def body(i, _):
            for a in (0, 1):
                for k in range(4):
                    left, right = tile(a, 0, i * 64, 64, k), tile(a, 1, i * 64, 64, k)
                    for t in range(PANELS):
                        p_cand[t, rows8(a * BS + i * 64, 64), k * 128 : (k + 1) * 128] = (
                            left * (in_col[t, 0] * present[a, 0])
                            + right * (in_col[t, 1] * present[a, 1])
                        )
            return 0

        lax.fori_loop(0, 8, body, 0)

    def build_rows():
        def body(i, _):
            lanes = pl.ds(pl.multiple_of(i * 128, 128), 128)
            for b in (0, 1):
                for k in range(4):
                    top, low = tile(0, b, i * 128, 128, k), tile(1, b, i * 128, 128, k)
                    for t in range(PANELS):
                        both = top * (in_row[t, 0] * present[0, b])
                        both = both + low * (in_row[t, 1] * present[1, b])
                        x_cand[t, b * BS + k * 128 : b * BS + (k + 1) * 128, lanes] = both.T
            return 0

        lax.fori_loop(0, 4, body, 0)

    d_paths = [
        crossing_path(links, lines, sibling, z, core, col, x, y, len(GROUPS[g]), *d_bufs[g])
        for g in range(3)
    ]
    d_out = [d_bufs[g][-1] for g in range(3)]

    spots = ((x, y), (y, x))

    def p_piece(h):
        return lambda k: p_cand.at[:, rows8(h * BS + k * 128, 128), :]

    def p_piece2(h):
        a = spots[h][0]
        return lambda k: p_cand.at[:, rows8(h * BS + a * 128 + k * 32, 32), :]

    p_level1 = [lines[h].scatter_ring(p_piece(h), half_rows, p_near.at[h], p_far.at[h]) for h in (0, 1)]
    p_level2 = [
        lines[1 - h].scatter_ring(p_piece2(h), half_rows, p_near2.at[h], p_far2.at[h])
        for h in (0, 1)
    ]

    def add_far(h, line, base, size, far):
        for w, d in ((0, 1), (1, 3)):
            at = rows8(base + line.spot[d] * size + w * (size // 2), size // 2)
            p_cand[:, at, :] = p_cand[:, at, :] + far[h, w]

    def add_near(h, line, base, size, near):
        at = rows8(base + line.me * size, size)
        p_cand[:, at, :] = p_cand[:, at, :] + near[h, 0] + near[h, 1]

    def p0():
        for h in (0, 1):
            start(p_level1[h][0])

    def p1():
        for h in (0, 1):
            arrive(p_level1[h][0])
            add_far(h, lines[h], h * BS, 128, p_far)
            start(p_level1[h][1])

    def p2():
        for h in (0, 1):
            arrive(p_level1[h][1])
            add_near(h, lines[h], h * BS, 128, p_near)
            start(p_level2[h][0])

    def p3():
        for h in (0, 1):
            arrive(p_level2[h][0])
            add_far(h, lines[1 - h], h * BS + spots[h][0] * 128, 32, p_far2)
            start(p_level2[h][1])

    def p4():
        for h in (0, 1):
            arrive(p_level2[h][1])
            at = rows8(h * BS + spots[h][0] * 128 + spots[h][1] * 32, 32)
            slices[:, h * 32 : (h + 1) * 32, :] = (
                p_cand[:, at, :] + p_near2[h, 0] + p_near2[h, 1]
            )

    p_path = [p0, p1, p2, p3, p4]

    up, down = (zs[1] * 2 + core, col), (zs[7] * 2 + core, col)
    x_swap = [
        links.copy(lambda: x_cand.at[:, rows8((1 - core) * BS, BS), :], lambda: x_sib, sibling)
    ]

    def x_piece(k, first=0, size=64):
        return x_sib.at[:, rows8(k * 64 + first, size), :]

    x_steps = []
    for i in range(4):
        size = 32 if i == 0 else 64
        x_steps.append(
            [
                links.copy(
                    lambda w=w, i=i, size=size: x_piece(
                        zs[4 - i if w == 0 else 4 + i], 32 * w if i == 0 else 0, size
                    ),
                    lambda w=w, i=i, size=size: x_ring.at[w, i, :, pl.ds(0, size), :],
                    up if w == 0 else down,
                )
                for w in (0, 1)
            ]
        )

    def x0():
        start(x_swap)

    def x1():
        arrive(x_swap)
        x_sib[...] = x_sib[...] + x_cand[:, rows8(core * BS, BS), :]
        start(x_steps[0])

    def x_next(i):
        def run():
            arrive(x_steps[i - 1])
            first, size = (32, 32) if i == 1 else (0, 64)
            for w in (0, 1):
                number = zs[4 - i if w == 0 else 4 + i]
                at = rows8(number * 64 + first * w, size)
                x_sib[:, at, :] = x_sib[:, at, :] + x_ring[w, i - 1, :, :size, :]
            start(x_steps[i])

        return run

    def x5():
        arrive(x_steps[3])
        slices[:, 64:, :] = x_sib[:, rows8(z * 64, 64), :] + x_ring[0, 3] + x_ring[1, 3]

    x_path = [x0, x1, x_next(1), x_next(2), x_next(3), x5]

    def gather_path(first_panel, count, sem):
        panels = pl.ds(first_panel, count)

        def c_piece(h):
            return lambda k: c_row.at[panels, rows8(h * BS + k * 128, 128), :]

        def c_piece2(h):
            a = spots[h][0]
            return lambda k: c_row.at[panels, rows8(h * BS + a * 128 + k * 32, 32), :]

        def own_rows(h):
            return lambda: slices.at[panels, pl.ds(h * 32, 32), :]

        level2 = [
            lines[1 - h].gather_ring(own_rows(h), c_piece2(h), half_rows) for h in (0, 1)
        ]
        level1 = [
            lines[h].gather_ring(lambda h=h: c_piece(h)(lines[h].me), c_piece(h), half_rows)
            for h in (0, 1)
        ]

        def y_piece(k, first=0, size=64):
            return c_col.at[panels, rows8(core * BS + k * 64 + first, size), :]

        y_own = lambda: slices.at[panels, pl.ds(64, 64), :]
        y_steps = []
        for i in range(4):
            copies = []
            for w in (0, 1):
                first, size = (32 * w, 32) if i == 3 else (0, 64)
                number = zs[(8 - i) % 8 if w == 0 else i]

                def dst(number=number, first=first, size=size):
                    return y_piece(number, first, size)

                copies.append(links.copy(y_own if i == 0 else dst, dst, up if w == 0 else down))
            y_steps.append(copies)
        mine = lambda: c_col.at[panels, rows8(core * BS, BS), :]
        y_back = [links.copy(mine, mine, sibling)]

        def keep(n):
            if n < 2:
                src, dst = own_rows(n)(), c_piece2(n)(spots[n][1])
            else:
                src, dst = y_own(), y_piece(z)
            return pltpu.make_async_copy(src, dst, own_sem.at[sem + n])

        def r0():
            for h in (0, 1):
                keep(h).start()
                start(level2[h][0])

        def r1():
            for h in (0, 1):
                arrive(level2[h][0])
                start(level2[h][1])

        def r2():
            for h in (0, 1):
                keep(h).wait()
                arrive(level2[h][1])
                start(level1[h][0])

        def r3():
            for h in (0, 1):
                arrive(level1[h][0])
                start(level1[h][1])

        def r4():
            for h in (0, 1):
                arrive(level1[h][1])

        def y0():
            keep(2).start()
            start(y_steps[0])

        def y_next(i):
            def run():
                arrive(y_steps[i - 1])
                start(y_steps[i])

            return run

        def y4():
            keep(2).wait()
            arrive(y_steps[3])
            start(y_back)

        def y5():
            arrive(y_back)

        return [r0, r1, r2, r3, r4], [y0, y_next(1), y_next(2), y_next(3), y4, y5]

    ra, ya = gather_path(0, 1, 0)
    rb, yb = gather_path(1, 2, 3)

    sub = lax.broadcasted_iota(jnp.int32, (STRIP, 128), 0)
    lane = lax.broadcasted_iota(jnp.int32, (STRIP, 128), 1)
    shape = (STRIP, 128)

    def window(r0, k, count=1):
        return pl.ds(pl.multiple_of(r0 + k * 128, 128), count * 128)

    def strip_step(r0, i):
        rr = pl.multiple_of(r0 + i * STRIP, STRIP)
        strip = [work[pl.ds(rr, STRIP), window(r0, k)] for k in range(5)]
        column = [
            jnp.broadcast_to(strip[0][:, i * STRIP + j : i * STRIP + j + 1], shape)
            for j in range(STRIP)
        ]
        for j in range(STRIP):
            scale = lax.rsqrt(jnp.broadcast_to(column[j][j : j + 1, :], shape))
            solved = column[j] * scale
            below = jnp.where(sub > j, solved, 0.0)
            for k in range(j + 1, STRIP):
                column[k] = column[k] - below * jnp.broadcast_to(solved[k : k + 1, :], shape)
            for k in range(5):
                line = jnp.broadcast_to(strip[k][j : j + 1, :], shape) * scale
                strip[k] = jnp.where(sub == j, line, strip[k] - below * line)
        strip[0] = jnp.where(lane >= sub + i * STRIP, strip[0], 0.0)
        for k in range(5):
            work[pl.ds(rr, STRIP), window(r0, k)] = strip[k]
        if i < 128 // STRIP - 1:
            ph, plow = split(jnp.concatenate(strip, axis=1))
            dh, dl = split(strip[0])
            left = jnp.concatenate([dh, dh, dl], axis=0)
            right = jnp.concatenate([ph, plow, ph], axis=0)
            change = contract(left, right, 0, 0)
            at = pl.ds(rr + STRIP, 128 - (i + 1) * STRIP)
            for k in range(5):
                lanes = window(r0, k)
                work[at, lanes] = (
                    work[at, lanes] - change[(i + 1) * STRIP :, k * 128 : (k + 1) * 128]
                )

    def factor(events):
        eye_row = lax.broadcasted_iota(jnp.int32, (64, 128), 0)
        eye_lane = lax.broadcasted_iota(jnp.int32, (64, 128), 1)
        for i in range(8):
            work[i * 64 : (i + 1) * 64, BS:] = jnp.zeros((64, BS), F32)
            first = (i // 2) * 128
            work[i * 64 : (i + 1) * 64, BS + first : BS + first + 128] = jnp.where(
                eye_row + (i % 2) * 64 == eye_lane, 1.0, 0.0
            )

        def outer(o, _):
            r0 = pl.multiple_of(o * 128, 128)
            for i in range(128 // STRIP):
                if i % 2 == 0:
                    for k in range(4):
                        todo = events[k * 2 + i // 2]
                        if todo:

                            @pl.when(o == k)
                            def _(todo=todo):
                                for event in todo:
                                    event()

                strip_step(r0, i)
            ph, plow = split(work[pl.ds(r0, 128), window(r0, 0, 5)])
            right = jnp.concatenate([ph, plow, ph], axis=0)
            for k in range(1, 4):

                @pl.when(k > o)
                def _(k=k):
                    lh, ll = split(work[pl.ds(r0, 128), k * 128 : (k + 1) * 128])
                    left = jnp.concatenate([lh, lh, ll], axis=0)
                    at, lanes = pl.ds(k * 128, 128), window(r0, 0, 5)
                    work[at, lanes] = work[at, lanes] - contract(left, right, 0, 0)

            return 0

        lax.fori_loop(0, 4, outer, 0)

    def piece(g, n, i):
        return d_out[g][i // 2, n * 256 + (i % 2) * 128 : n * 256 + (i % 2) * 128 + 128, :]

    def save(t):
        copies = [pltpu.make_async_copy(work.at[:, pl.ds(0, BS)], u_out.at[t], own_sem.at[6 + t])]
        if t == 2:
            copies.append(pltpu.make_async_copy(work.at[:, pl.ds(BS, BS)], w_out, own_sem.at[9]))
        return copies

    def keep_factor(t):
        for k in range(1, 4):
            work[k * 128 : (k + 1) * 128, : k * 128] = jnp.zeros((128, k * 128), F32)
        for copy in save(t):
            copy.start()
        if t < 2:
            for i in range(4):
                at = pl.ds(i * 128, 128)
                inv_h[t, at, :], inv_l[t, at, :] = split(work[at, BS:])

    def solve_crossing(n, t, source):
        for i in range(4):
            bh, bl = split(source(i))
            part = (
                contract(inv_h[t], bh, 1, 1)
                + contract(inv_h[t], bl, 1, 1)
                + contract(inv_l[t], bh, 1, 1)
            )
            lanes = pl.ds(i * 128, 128)
            cross_h[n, :, lanes], cross_l[n, :, lanes] = split(part)

    def pair(first, second, i):
        lanes = pl.ds(i * 128, 128)
        ah, al = cross_h[first, :, lanes], cross_l[first, :, lanes]
        return (
            contract(ah, cross_h[second], 0, 0)
            + contract(ah, cross_l[second], 0, 0)
            + contract(al, cross_h[second], 0, 0)
        )

    def thin(rows, high, low, axis):
        ah, al = split(rows)
        return contract(ah, high, 1, axis) + contract(ah, low, 1, axis) + contract(al, high, 1, axis)

    build_crossing((0,))
    pl.semaphore_wait(barrier, len(places))
    d0, d1, d2 = d_paths
    px, xx = p_path, x_path
    d0[0]()
    d0[1]()
    build_crossing((1,))
    d1[0]()
    build_rows()
    d0[2]()
    xx[0]()
    d1[1]()
    build_crossing((2,))
    d0[3]()
    d2[0]()
    build_columns()
    d0[4]()
    xx[1]()
    d0[5]()
    d1[2]()
    d0[6]()
    d1[3]()
    d0[7]()
    xx[2]()
    d1[4]()
    d0[8]()
    for i in range(4):
        work[i * 128 : (i + 1) * 128, :BS] = piece(0, 0, i)
    factor(
        [
            [d2[1]],
            [d1[5]],
            [xx[3]],
            [d1[6]],
            [d2[2], px[0]],
            [xx[4]],
            [d1[7], d2[3]],
            [],
        ]
    )
    d1[8]()
    keep_factor(0)
    solve_crossing(0, 0, lambda i: piece(1, 0, i))
    for copy in save(0):
        copy.wait()
    for i in range(4):
        work[i * 128 : (i + 1) * 128, :BS] = piece(1, 1, i) - pair(0, 0, i)

    def first_panel():
        slices[0] = thin(slices[0], inv_h[0], inv_l[0], 1)
        ra[0]()
        ya[0]()

    factor(
        [
            [d2[4], px[1]],
            [xx[5]],
            [d2[5]],
            [],
            [d2[6]],
            [px[2]],
            [px[3]],
            [d2[7], px[4], first_panel],
        ]
    )
    ra[1]()
    d2[8]()
    keep_factor(1)
    solve_crossing(1, 0, lambda i: piece(2, 0, i))
    solve_crossing(2, 1, lambda i: piece(2, 1, i) - pair(1, 0, i))
    slices[1] = thin(
        slices[1] - thin(slices[0], cross_h[0], cross_l[0], 0), inv_h[1], inv_l[1], 1
    )
    slices[2] = (
        slices[2]
        - thin(slices[0], cross_h[1], cross_l[1], 0)
        - thin(slices[1], cross_h[2], cross_l[2], 0)
    )
    rb[0]()
    yb[0]()
    for copy in save(1):
        copy.wait()
    for i in range(4):
        work[i * 128 : (i + 1) * 128, :BS] = piece(2, 2, i) - pair(1, 1, i) - pair(2, 2, i)
    factor(
        [
            [ya[1], ra[2]],
            [rb[1], yb[1]],
            [ya[2], ra[3]],
            [rb[2]],
            [yb[2], ya[3]],
            [ra[4]],
            [yb[3], ya[4]],
            [rb[3], ya[5]],
        ]
    )
    keep_factor(2)
    yb[4]()
    rb[4]()
    yb[5]()
    for copy in save(2):
        copy.wait()
    links.drain()


def eliminate(pattern, order, m):
    vmem = pl.BlockSpec(memory_space=pltpu.VMEM)
    whole = pl.BlockSpec(memory_space=pl.ANY)
    smem = pl.BlockSpec(memory_space=pltpu.SMEM)
    d_shapes = []
    for group in GROUPS:
        rows = len(group) * 256
        d_shapes.append(
            (
                pltpu.VMEM((2, rows, BS), F32),
                pltpu.VMEM((rows, BS), F32),
                pltpu.VMEM((2, 3, rows // 8, BS), F32),
                pltpu.VMEM((2, rows // 8, BS), F32),
                pltpu.VMEM((2, 3, rows // 32, BS), F32),
                pltpu.VMEM((rows // 16, BS), F32),
                pltpu.VMEM((7, rows // 32, 128), F32),
                pltpu.VMEM((rows // 16, BS), F32),
                pltpu.VMEM((2, rows, BS), F32),
            )
        )
    return pl.pallas_call(
        front_kernel,
        out_shape=(
            jax.ShapeDtypeStruct((PANELS, 2 * BS, BS), F32),
            jax.ShapeDtypeStruct((PANELS, 2 * BS, BS), F32),
            jax.ShapeDtypeStruct((PANELS, BS, BS), F32),
            jax.ShapeDtypeStruct((BS, BS), F32),
        ),
        in_specs=[smem, smem, vmem],
        out_specs=(whole, whole, whole, whole),
        scratch_shapes=[
            pltpu.VMEM((PANELS, 2 * BS, BS), F32),
            pltpu.VMEM((2, 2, PANELS, 64, BS), F32),
            pltpu.VMEM((2, 2, PANELS, 128, BS), F32),
            pltpu.VMEM((2, 2, PANELS, 16, BS), F32),
            pltpu.VMEM((2, 2, PANELS, 32, BS), F32),
            pltpu.VMEM((PANELS, 2 * BS, BS), F32),
            pltpu.VMEM((PANELS, BS, BS), F32),
            pltpu.VMEM((2, 4, PANELS, 64, BS), F32),
            pltpu.VMEM((PANELS, 128, BS), F32),
            tuple(d_shapes),
            pltpu.VMEM((BS, 2 * BS), F32),
            pltpu.VMEM((2, BS, BS), jnp.bfloat16),
            pltpu.VMEM((2, BS, BS), jnp.bfloat16),
            pltpu.VMEM((3, BS, BS), jnp.bfloat16),
            pltpu.VMEM((3, BS, BS), jnp.bfloat16),
            pltpu.SemaphoreType.DMA((10,)),
            pltpu.SemaphoreType.DMA((SEMAPHORES,)),
            pltpu.SemaphoreType.DMA((SEMAPHORES,)),
        ],
        compiler_params=pltpu.CompilerParams(
            collective_id=0, has_side_effects=True, vmem_limit_bytes=62 * 1024 * 1024
        ),
    )(pattern, order, m)


def update_kernel(pattern_ref, order_ref, m_in, row_in, col_in, u_in, w_in, out,
                  m, solved_in, u_all, w_last, high, low, sems):
    sources = (row_in, col_in)
    loads = {"w": pltpu.make_async_copy(w_in, w_last, sems.at[0])}
    for n, (t, side) in enumerate(((2, 0), (2, 1), (0, 0), (0, 1), (1, 0), (1, 1))):
        loads[t, side] = pltpu.make_async_copy(
            sources[side].at[t], solved_in.at[side, t], sems.at[1 + n]
        )
    loads["m"] = pltpu.make_async_copy(m_in, m, sems.at[7])
    loads["u"] = pltpu.make_async_copy(u_in, u_all, sems.at[8])
    for load in loads.values():
        load.start()
    loads["w"].wait()
    for side in (0, 1):
        loads[2, side].wait()
        high[side, 2], low[side, 2] = split(product(solved_in[side, 2], w_last[...], 1, 1))
    for t in (0, 1):
        for side in (0, 1):
            loads[t, side].wait()
            high[side, t], low[side, t] = split(solved_in[side, t])
    loads["m"].wait()
    loads["u"].wait()

    row, col = lax.axis_index("row"), lax.axis_index("col")
    row_ids, col_ids = (row, 16 + row), (col, 16 + col)

    def turn(number):
        found = jnp.int32(PANELS)
        for t in reversed(range(PANELS)):
            found = jnp.where(order_ref[t] == number, t, found)
        return found

    def tile_rows(a, b, k, u=0, n=BS):
        return pl.ds((a * BS + u) * 8 + b * 4 + k, n, stride=8)

    def put(a, b, value):
        for k in range(4):
            out[tile_rows(a, b, k), :] = value[:, k * 128 : (k + 1) * 128]

    for a in (0, 1):
        for b in (0, 1):
            ra, cb = turn(row_ids[a]), turn(col_ids[b])
            rows, cols = pl.ds(a * BS, BS), pl.ds(b * BS, BS)

            @pl.when((ra == 3) & (cb == 3))
            def _(a=a, b=b, rows=rows, cols=cols):
                total = jnp.zeros((BS, BS), F32)
                for t in range(PANELS):
                    ch, cl = high[0, t, rows, :], low[0, t, rows, :]
                    rh, rl = high[1, t, cols, :], low[1, t, cols, :]
                    total = total + contract(ch, rh, 1, 1)
                    total = total + contract(ch, rl, 1, 1)
                    total = total + contract(cl, rh, 1, 1)
                present = pattern_ref[row_ids[a], col_ids[b]].astype(F32)
                for k in range(4):
                    at = tile_rows(a, b, k)
                    old = m[at, :] * present
                    out[at, :] = old - total[:, k * 128 : (k + 1) * 128]

            def solved(side, t, at):
                return high[side, t, at, :].astype(F32) + low[side, t, at, :].astype(F32)

            for t in range(PANELS):

                @pl.when((ra == t) & (cb == t))
                def _(a=a, b=b, t=t):
                    put(a, b, u_all[t].T)

                @pl.when((cb == t) & (ra > t))
                def _(a=a, b=b, t=t, rows=rows):
                    put(a, b, solved(0, t, rows))

                @pl.when((ra == t) & (cb > t))
                def _(a=a, b=b, t=t, cols=cols):
                    put(a, b, solved(1, t, cols).T)


def update(pattern, order, m, c_row, c_col, u_all, w_last):
    vmem = pl.BlockSpec(memory_space=pltpu.VMEM)
    smem = pl.BlockSpec(memory_space=pltpu.SMEM)
    return pl.pallas_call(
        update_kernel,
        out_shape=jax.ShapeDtypeStruct(m.shape, F32),
        in_specs=[smem, smem] + [pl.BlockSpec(memory_space=pl.ANY)] * 5,
        out_specs=vmem,
        scratch_shapes=[
            pltpu.VMEM(m.shape, F32),
            pltpu.VMEM((2, PANELS, 2 * BS, BS), F32),
            pltpu.VMEM((PANELS, BS, BS), F32),
            pltpu.VMEM((BS, BS), F32),
            pltpu.VMEM((2, PANELS, 2 * BS, BS), jnp.bfloat16),
            pltpu.VMEM((2, PANELS, 2 * BS, BS), jnp.bfloat16),
            pltpu.SemaphoreType.DMA((9,)),
        ],
        compiler_params=pltpu.CompilerParams(vmem_limit_bytes=58 * 1024 * 1024),
    )(pattern, order, m, c_row, c_col, u_all, w_last)


def per_device(front_values, block_pattern, panel_order):
    m = front_values.reshape(8192, 128)
    solved = eliminate(block_pattern, panel_order, m)
    return update(block_pattern, panel_order, m, *solved).reshape(front_values.shape)


def solution(mesh):
    return jax.shard_map(
        per_device,
        mesh=mesh,
        in_specs=(P(None, "row", None, None, "col", None), P(), P()),
        out_specs=P(None, "row", None, None, "col", None),
        check_vma=False,
    )
```
